32 devices in a mesh: groups: 2 (over y), dom: 4 (over z), cls: 2 (over x), coef: 2 (over core).
Axes of the slice: x: 2, y: 2, z: 4, core: 2. Of those that a mesh axis runs over, the one named last changes fastest.
Arguments:
- particles: bfloat16 [3584, 2, 5120], P(('groups', 'dom', 'cls'), None, 'coef'), parts along dimension 0, may hold values from -6 to 6
- classes: int32 [3584, 1], P(('groups', 'dom', 'cls')), parts along dimension 0, may hold values from 0 to 255; in each aligned block of 224 rows (0 to 223, 224 to 447, ...) at most 2 rows name the same one
- angles: int32 [3584], P(('groups', 'dom', 'cls')), parts along dimension 0, may hold values from 0 to 359
- counts: int32 [3584], P(('groups', 'dom', 'cls')), parts along dimension 0, may hold values from 1 to 8
Outputs:
- averages: bfloat16 [512, 2, 5120], P(('groups', 'dom', 'cls'), None, 'coef'), parts along dimension 0
- gains: float32 [3584], P(('groups', 'dom', 'cls')), parts along dimension 0
The draws below stay inside these ranges and needn't reach their ends.
There are 2 independent parts, one for each index of `groups`. The reference program is written for one: setup_inputs(seed, part) draws one part's arguments, and reference() takes and returns one part's arrays. A program takes and returns all parts, laid end to end along the dimension named above; each array names one. Nothing has to cross between parts.
Inputs may be any that keep to these rules, and one draw needn't show every extreme that they name: `classes`: in each device's aligned block of 224 particles no class holds more than 2 particles, and some class holds exactly 2; every class holds at least one particle of the part.
All inputs are finite; a program needn't handle non-finite values.
Results may differ from the reference program's by a relative error of at most 0.0014.
Values may be sent and summed in bfloat16 or wider, within the bound.
No kernel may reach another device: no remote copies, remote signals or barrier semaphores. Data moves between devices by JAX's collectives and lax.ppermute only.
A program may use at most 64 MiB of HBM per device.

```python
import math
import jax
import jax.numpy as jnp
import numpy as np
from jax import lax

NK = 80
NQ = 64
NC = 5120
CLASSES = 256
CAP = 2
P_DEV = 224
PARTICLES = 1792


def touch_ends(result, key, low, top_value):
    place = [jax.random.randint(jax.random.fold_in(key, axis), (), 0, length) for axis, length in enumerate(result.shape)]
    main_axis = result.shape.index(max(result.shape))
    neighbour = place[:main_axis] + [(place[main_axis] + 1) % result.shape[main_axis]] + place[main_axis + 1:]
    return result.at[tuple(place)].set(low).at[tuple(neighbour)].set(top_value)


def block_scale(rng, shape, split, least, largest):
    level = 1.0
    for position, blocks in split:
        heights = jax.random.uniform(jax.random.fold_in(jax.random.fold_in(rng, 6), position), (blocks,), jnp.float32, least / len(split), largest / len(split))
        level = level * jnp.repeat(jnp.exp(heights), shape[position] // blocks).reshape((-1,) + (1,) * (len(shape) - 1 - position))
    return level


def deal_out(own_key, own, number, rows, number_of, top, reach, lean):
    sequence = jax.random.permutation(own_key, number_of)
    crowded, ordinary = shares(number_of, rows * top, reach, lean, True), shares(number_of, rows * top, reach, lean, False)
    places = jnp.arange(number_of)

    def named(tallies, turn):
        used = int((tallies > 0).sum())
        fixed = max(1, used // 4)
        shifted = fixed + (places - fixed + turn * (used - fixed)) % max(1, number_of - fixed)
        return jnp.zeros((number_of,), jnp.int32).at[sequence[jnp.where(places < fixed, places, shifted)]].set(jnp.asarray(tallies, jnp.int32))

    tallies = jnp.where(number % 4 == 0, named(crowded, number // 4), named(ordinary, number - number // 4 - 1))
    mixed = jax.random.permutation(jax.random.fold_in(own, 3), number_of)
    source_of, taker = mixed[0:number_of // 2 * 2:2], mixed[1:number_of // 2 * 2:2]
    slack = jnp.minimum(tallies[source_of] - 1, reach - tallies[taker]) // 2
    slack = jnp.where((source_of == sequence[0]) | (taker == sequence[0]) | (tallies[taker] == 0), 0, jnp.maximum(slack, 0))
    shifted = jax.random.randint(jax.random.fold_in(own, 4), (number_of // 2,), 0, 1 << 20) % (slack + 1)
    tallies = tallies.at[source_of].add(-shifted).at[taker].add(shifted)
    members = jnp.searchsorted(jnp.cumsum(tallies), jnp.arange(rows * top), side="right").astype(jnp.int32)
    listing = members.reshape(top, rows).T
    listing = listing[jax.random.permutation(jax.random.fold_in(own, 1), rows)]
    turn = jax.random.randint(jax.random.fold_in(own, 2), (rows, 1), 0, top)
    return jnp.take_along_axis(listing, (jnp.arange(top)[None, :] + turn) % top, axis=1)


def shares(amount, total, limit, slope, full):
    weights = [(1 << 20) // math.isqrt(standing ** slope) + 1 for standing in range(1, amount + 1)]
    largest = limit if full else min(limit, max(-(-total // amount), total * weights[0] // sum(weights)))
    least = 1 if total - largest >= amount - 1 else 0
    given, spare = [largest] + [least] * (amount - 1), total - largest - least * (amount - 1)
    while spare > 0:
        free = [i for i in range(1, amount) if given[i] < largest] or [i for i in range(1, amount) if given[i] < limit]
        mass, left = sum([weights[i] for i in free]), spare
        for i in free:
            more = min(limit - given[i], max(1, left * weights[i] // mass), spare)
            given[i] = given[i] + more
            spare = spare - more
    return np.array(given)


def bell_draw(stream_key, extent, deviation, most, cuts=(), held_as=jnp.bfloat16):
    gain = block_scale(stream_key, extent, cuts, -0.22, 0.18) if cuts else 1.0
    array = jax.random.normal(stream_key, extent, jnp.float32) * deviation * gain
    return jnp.minimum(jnp.maximum(array, -most), most).astype(held_as)


def setup_inputs(seed: int = 0, part: int = 0) -> dict:
    splits = jax.random.split(jax.random.key(seed), 5)
    part_splits = jax.random.split(jax.random.fold_in(splits[4], part), 5)
    particles = bell_draw(part_splits[0], (PARTICLES, 2, NC), 1.0, 6.0, ((0, 8), (2, 2)))
    classes_keys = jax.random.split(jax.random.fold_in(part_splits[1], 1), PARTICLES // P_DEV)
    classes_turns = jax.random.permutation(jax.random.fold_in(part_splits[1], 3), PARTICLES // P_DEV)
    classes = jax.vmap(lambda own, number: deal_out(jax.random.fold_in(part_splits[1], 2), own, number, P_DEV, CLASSES, 1, CAP, 2))(classes_keys, classes_turns).reshape((PARTICLES, 1))
    angles = touch_ends(jax.random.randint(part_splits[2], (PARTICLES,), 0, 360), jax.random.fold_in(part_splits[2], 1), 0, 359).astype(jnp.int32)
    counts = touch_ends(jax.random.randint(part_splits[3], (PARTICLES,), 1, 9), jax.random.fold_in(part_splits[3], 1), 1, 8).astype(jnp.int32)
    return dict(particles=particles, classes=classes, angles=angles, counts=counts)


def rotation(angle, first, count):
    frequency = first + jnp.arange(count, dtype=jnp.int32)
    turns = angle[..., None] * frequency % 360
    theta = turns.astype(jnp.float32) * (2.0 * math.pi / 360.0)
    return (jnp.cos(theta)[..., None], jnp.sin(theta)[..., None])

def reference(particles, classes, angles, counts):
    blocks = particles.shape[0] // P_DEV
    stacked = particles.reshape(blocks, P_DEV, 2, NK, NQ)
    labels = classes[:, 0].reshape(blocks, P_DEV)
    turned = angles.reshape(blocks, P_DEV)
    weights = counts.reshape(blocks, P_DEV)

    def accumulate(carry, item):
        values, label, angle, weight = item
        cosine, sine = rotation(angle, 0, NK)
        real_part = values[:, 0].astype(jnp.float32)
        imag_part = values[:, 1].astype(jnp.float32)
        factor = weight.astype(jnp.float32)[:, None, None]
        aligned = jnp.stack([factor * (real_part * cosine - imag_part * sine), factor * (real_part * sine + imag_part * cosine)], axis=1)
        sums = carry[0] + jax.ops.segment_sum(aligned, label, num_segments=CLASSES)
        totals = carry[1] + jax.ops.segment_sum(weight.astype(jnp.float32), label, num_segments=CLASSES)
        return ((sums, totals), None)
    initial = (jnp.zeros((CLASSES, 2, NK, NQ), jnp.float32), jnp.zeros((CLASSES,), jnp.float32))
    (sums, totals), unused = lax.scan(accumulate, initial, (stacked, labels, turned, weights))
    averages = (sums / totals[:, None, None, None]).astype(jnp.bfloat16)

    def score(item):
        values, label, angle = item
        cosine, sine = rotation(angle, 0, NK)
        real_part = values[:, 0].astype(jnp.float32)
        imag_part = values[:, 1].astype(jnp.float32)
        mean = jnp.take(averages, label, axis=0).astype(jnp.float32)
        mean_re = mean[:, 0]
        mean_im = mean[:, 1]
        back_re = mean_re * cosine + mean_im * sine
        back_im = mean_im * cosine - mean_re * sine
        term = 2.0 * (real_part * back_re + imag_part * back_im) - (mean_re * mean_re + mean_im * mean_im)
        return lax.optimization_barrier(jnp.sum(term, axis=(1, 2))) / math.sqrt(2.0 * NK * NQ)
    gains = lax.map(score, (stacked, labels, turned))
    return (averages.reshape(CLASSES, 2, NK * NQ), gains.reshape(-1))
```

```python
import functools
import math

import jax
import jax.numpy as jnp
from jax import lax
from jax.experimental import pallas as pl
from jax.experimental.pallas import tpu as pltpu
from jax.sharding import PartitionSpec as P

NK = 80
NQ = 64
CLASSES = 256
CAP = 2
LANES = 128
BLOCK = 256
SHARES = (0.5, 0.5)
PARAMS = pltpu.CompilerParams(vmem_limit_bytes=48 << 20)
NT = (((1,), (1,)), ((), ()))
f32 = jnp.float32
bf16 = jnp.bfloat16
i32 = jnp.int32


def matmul(a, b, dims=(((1,), (0,)), ((), ()))):
    return lax.dot_general(a, b, dims, preferred_element_type=f32)


def split(value):
    high = value.astype(bf16)
    return high, (value - high.astype(f32)).astype(bf16)


def split3(value):
    high = value.astype(bf16)
    rest = value - high.astype(f32)
    mid = rest.astype(bf16)
    return high, mid, (rest - mid.astype(f32)).astype(bf16)


def place_of(slot, count):
    rows = lax.broadcasted_iota(i32, (count, slot.shape[1]), 0)
    return jnp.where(rows == slot, 1.0, 0.0).astype(bf16)


def pack_first(parts, cap, meta_ref, x_ref, *out_refs):
    slot_ref = out_refs[parts]
    people = meta_ref.shape[1]
    width = x_ref.shape[1]
    meta = meta_ref[...]
    dest = meta[0:1]
    chosen = jnp.where(lax.broadcasted_iota(i32, (16, people), 0) == dest, 1.0, 0.0)
    before = jnp.where(
        lax.broadcasted_iota(i32, (people, people), 0) < lax.broadcasted_iota(i32, (people, people), 1), 1.0, 0.0
    ).astype(bf16)
    ahead = matmul(chosen.astype(bf16), before)
    rank = jnp.sum(chosen * ahead, axis=0, keepdims=True).astype(i32)
    over = jnp.max(jnp.where(rank >= cap, 1.0, 0.0))
    slot = jnp.where(rank < cap, dest * cap + rank, -1)
    slot_ref[...] = jnp.broadcast_to(jnp.where(rank < cap, dest * LANES + rank, -1), slot_ref.shape)
    half = lax.shift_right_logical(meta[2:3], 1)
    rows = lax.broadcasted_iota(i32, (LANES, people), 0)
    details = jnp.where(rows == 0, meta[1:2], 0)
    details = jnp.where(rows == 1, half, details)
    details = jnp.where(rows == 2, meta[2:3] - 2 * half, details)
    details = jnp.where(rows == 3, meta[3:4], details)
    details = details.astype(f32).astype(bf16)
    lane = lax.broadcasted_iota(i32, (cap, LANES), 1)
    for part in range(parts):
        place = place_of(slot - part * cap, cap)
        out_refs[part][:, :width] = matmul(place, x_ref[...]).astype(bf16)
        block = jnp.where(lane == 4, over, matmul(place, details, NT))
        out_refs[part][:, width:] = block.astype(bf16)


def pack_next(parts, cap, slot_ref, x_ref, *out_refs):
    slot = slot_ref[0:1]
    dest = lax.shift_right_arithmetic(slot, 7)
    slot = jnp.where(slot >= 0, dest * cap + (slot - dest * LANES), -1)
    for part in range(parts):
        out_refs[part][...] = matmul(place_of(slot - part * cap, cap), x_ref[...]).astype(bf16)


def align(parts, cap, subs, nfreq, first, freqs, start, *refs):
    width = freqs * NQ
    taken, refs = refs[:parts], refs[parts:]
    if first:
        core_ref, code_ref, sums_ref, high_ref, mid_ref, cos_ref, sin_ref, hot_ref, info_ref = refs
        core = core_ref[0, 0]
        details = jnp.concatenate([ref[:, 2 * width :] for ref in taken], axis=0)
        columns = details.astype(f32)
        angle = 2.0 * columns[:, 1:2] + columns[:, 2:3]
        rows = parts * cap
        lane = lax.broadcasted_iota(i32, (rows, cos_ref.shape[1]), 1)
        third = jnp.where(lane >= nfreq, 1, 0) + jnp.where(lane >= 2 * nfreq, 1, 0)
        frequency = (lane - third * nfreq + core * nfreq).astype(f32)
        turns = angle * frequency
        turns = turns - 360.0 * jnp.floor((turns + 0.5) * (1.0 / 360.0))
        theta = turns * (2.0 * math.pi / 360.0)
        for table, ref in ((jnp.cos(theta), cos_ref), (jnp.sin(theta), sin_ref)):
            high, mid, low = [piece.astype(f32) for piece in split3(table)]
            ref[...] = jnp.where(third == 0, high, jnp.where(third == 1, mid, low)).astype(bf16)
        pick = jnp.where(
            lax.broadcasted_iota(i32, (16, LANES), 0) == lax.broadcasted_iota(i32, (16, LANES), 1), 1.0, 0.0
        ).astype(bf16)
        flat = matmul(pick, details, NT)
        hot = jnp.where(lax.broadcasted_iota(i32, (subs, rows), 0) == flat[0:1].astype(i32), 1.0, 0.0)
        hot_ref[0] = hot.astype(bf16)
        weighted = hot * flat[3:4]
        hot_ref[1] = weighted.astype(bf16)
        totals = jnp.sum(weighted, axis=1, keepdims=True)
        over = jnp.max(flat[4:5])
        slot = lax.broadcasted_iota(i32, info_ref.shape, 1)
        info_ref[...] = jnp.where(slot == 1, totals, jnp.where(slot == 2, over, 0.0))
    else:
        cos_ref, sin_ref, hot_ref, code_ref, sums_ref, high_ref, mid_ref = refs
        info_ref = None
    lanes = cos_ref.shape[1]
    weights = hot_ref[1]
    cosines, sines = cos_ref[...], sin_ref[...]
    row = lax.broadcasted_iota(i32, (lanes, BLOCK), 0)
    row = row - jnp.where(row >= nfreq, nfreq, 0) - jnp.where(row >= 2 * nfreq, nfreq, 0)
    lane_freq = lax.shift_right_logical(lax.broadcasted_iota(i32, (lanes, BLOCK), 1), 6)
    inside = lax.broadcasted_iota(i32, (lanes, BLOCK), 0) < 3 * nfreq
    for block in range(width // BLOCK):
        at = pl.ds(block * BLOCK, BLOCK)
        at_im = pl.ds(width + block * BLOCK, BLOCK)
        spread = jnp.where(inside & (row == lane_freq + (start + block * (BLOCK // NQ))), 1.0, 0.0).astype(bf16)
        cosine, sine = matmul(cosines, spread), matmul(sines, spread)
        real = jnp.concatenate([ref[:, at] for ref in taken], axis=0).astype(f32)
        imag = jnp.concatenate([ref[:, at_im] for ref in taken], axis=0).astype(f32)
        for here, value in ((at, real * cosine - imag * sine), (at_im, real * sine + imag * cosine)):
            high, mid = split(value)
            high_ref[:, here] = high
            mid_ref[:, here] = mid
            sums_ref[:, here] = matmul(weights, high) + matmul(weights, mid)
    largest = jnp.maximum(jnp.max(jnp.abs(sums_ref[...]), axis=1, keepdims=True), 1e-30)
    level = jnp.ceil(jnp.log(largest) * (4.0 / math.log(2.0)) + 0.02)
    coded = jnp.floor(sums_ref[...] * jnp.exp2(15.0 - 0.25 * level) + 0.5)
    code_ref[:, : 2 * width] = coded.astype(i32).astype(jnp.int16)
    slot = lax.broadcasted_iota(i32, (subs, LANES), 1)
    extra = jnp.where(slot == 0, level, 0.0 if info_ref is None else info_ref[...])
    code_ref[:, 2 * width :] = extra.astype(i32).astype(jnp.int16)


def score(parts, cap, others, first, last, *refs):
    codes, refs = refs[:others], refs[others:]
    sums_ref, high_ref, mid_ref, hot_ref, info_ref, refs = *refs[:5], refs[5:]
    if first:
        mean_ref, total_ref, gain_ref = refs
        info = info_ref[...]
        for code_ref in codes:
            more = code_ref[:, sums_ref.shape[1] :].astype(i32).astype(f32)
            slot = lax.broadcasted_iota(i32, more.shape, 1)
            info = info + jnp.where(slot == 0, 0.0, more)
        total_ref[...] = info
        so_far = None
    else:
        so_far_ref, mean_ref, gain_ref = refs
        info = info_ref[...]
        so_far = so_far_ref[0:1]
    wide = sums_ref.shape[1]
    sums = sums_ref[...]
    for code_ref in codes:
        level = code_ref[:, wide:].astype(i32).astype(f32)[:, 0:1]
        sums = sums + code_ref[:, :wide].astype(i32).astype(f32) * jnp.exp2(0.25 * level - 15.0)
    mean = (sums / info[:, 1:2]).astype(bf16)
    mean_ref[...] = mean
    wide_mean = mean.astype(f32)
    norm = jnp.sum(wide_mean * wide_mean, axis=1, keepdims=True)
    product = matmul(mean, high_ref[...], NT) + matmul(mean, mid_ref[...], NT)
    gain = jnp.sum(hot_ref[0].astype(f32) * (2.0 * product - norm), axis=0, keepdims=True)
    if so_far is not None:
        gain = gain + so_far
    if last:
        gain_ref[...] = jnp.zeros(gain_ref.shape, f32)
        for part in range(parts):
            gain_ref[part : part + 1, :cap] = gain[:, part * cap : (part + 1) * cap]
    else:
        gain_ref[...] = jnp.broadcast_to(gain, gain_ref.shape)


def unpack(parts, slot_ref, *refs):
    returned, out_ref = refs[:parts], refs[parts]
    slot = slot_ref[0:1]
    total = jnp.zeros((8, slot.shape[1]), f32)
    for part in range(parts):
        place = place_of(slot - part * LANES, LANES)
        mine = jnp.broadcast_to(returned[part][part : part + 1], (8, LANES))
        for piece in split3(mine):
            total = total + matmul(piece, place)
    out_ref[...] = total[0:1] * (1.0 / math.sqrt(2.0 * NK * NQ))


def call(kernel, outs, *args):
    shapes = [jax.ShapeDtypeStruct(shape, dtype) for shape, dtype in outs]
    return pl.pallas_call(kernel, out_shape=shapes, compiler_params=PARAMS)(*args)


def exchange(cap, particles, meta, square, n_dom, n_cls, pair):
    people, _, width = particles.shape
    axes = ("dom", "cls")
    parts = pair * n_cls
    groups = n_dom // pair
    owned = CLASSES // (n_dom * n_cls)
    subs = groups * owned
    rows = parts * cap
    nfreq = width // NQ
    step = BLOCK // NQ
    sizes = [max(step, int(nfreq * share) // step * step) for share in SHARES[:-1]]
    sizes.append(nfreq - sum(sizes))
    devices = [(z, x) for z in range(n_dom) for x in range(n_cls)]

    def forward(part):
        dz, dx = divmod(part, n_cls)
        return [(z * n_cls + x, (z ^ dz) * n_cls + (x + dx) % n_cls) for z, x in devices]

    def across(turn):
        return [(z * n_cls + x, ((z // pair + turn) % groups * pair + z % pair) * n_cls + x) for z, x in devices]

    def deliver(packed):
        sent = [lax.ppermute(packed[part], axes, forward(part)) for part in range(1, parts)]
        return [packed[0], *sent]

    lanes = -(-3 * nfreq // LANES) * LANES
    starts = [sum(sizes[:i]) for i in range(len(sizes))]
    core = lax.axis_index("coef").reshape(1, 1).astype(i32)
    arrived = []
    slot = None
    for number, (start, freqs) in enumerate(zip(starts, sizes)):
        x = particles[:, :, start * NQ : (start + freqs) * NQ].reshape(people, 2 * freqs * NQ)
        if number == 0:
            *packed, slot = call(
                functools.partial(pack_first, parts, cap),
                [((cap, 2 * freqs * NQ + LANES), bf16)] * parts + [((8, people), i32)],
                meta,
                x,
            )
        else:
            packed = call(
                functools.partial(pack_next, parts, cap), [((cap, 2 * freqs * NQ), bf16)] * parts, slot, x
            )
        arrived.append(deliver(packed))
    aligned = []
    for number, (start, freqs) in enumerate(zip(starts, sizes)):
        wide = 2 * freqs * NQ
        kernel = functools.partial(align, parts, cap, subs, nfreq, number == 0, freqs, start)
        outs = [
            ((subs, wide + LANES), jnp.int16),
            ((subs, wide), f32),
            ((rows, wide), bf16),
            ((rows, wide), bf16),
        ]
        if number == 0:
            more = [((rows, lanes), bf16)] * 2 + [((2, subs, rows), bf16), ((subs, LANES), f32)]
            specs = [pl.BlockSpec(memory_space=pltpu.VMEM)] * parts + [pl.BlockSpec(memory_space=pltpu.SMEM)]
            code, sums, high, mid, cosines, sines, hot, info = pl.pallas_call(
                kernel,
                in_specs=specs,
                out_shape=[jax.ShapeDtypeStruct(*out) for out in outs + more],
                compiler_params=PARAMS,
            )(*arrived[0], core)
        else:
            code, sums, high, mid = call(kernel, outs, *arrived[number], cosines, sines, hot)
        codes = [lax.ppermute(code, axes, across(turn)) for turn in range(1, groups)]
        aligned.append((codes, sums, high, mid))
    means = []
    gain = None
    for number, (codes, sums, high, mid) in enumerate(aligned):
        first, last = number == 0, number == len(sizes) - 1
        kernel = functools.partial(score, parts, cap, groups - 1, first, last)
        outs = [(sums.shape, bf16)]
        outs += [((subs, LANES), f32)] if first else []
        outs += [((-(-parts // 8) * 8, LANES), f32) if last else ((8, rows), f32)]
        args = [*codes, sums, high, mid, hot, info]
        if first:
            mean, *rest = call(kernel, outs, *args)
            info = rest[0]
            gain = rest[1]
        else:
            mean, gain = call(kernel, outs, *args, gain)
        means.append(mean)
    gain = lax.psum(gain, "coef")
    returned = [gain]
    for part in range(1, parts):
        returned.append(lax.ppermute(gain, axes, [(b, a) for a, b in forward(part)]))
    (gains,) = call(functools.partial(unpack, parts), [((1, people), f32)], slot, *returned)
    mine = [
        lax.dynamic_slice_in_dim(mean, square * owned, owned).reshape(owned, 2, -1) for mean in means
    ]
    averages = jnp.concatenate(mine, axis=2)
    return averages, gains.reshape(people), info[0, 2] > 0.0


def shards(particles, classes, angles, counts):
    n_dom = lax.axis_size("dom")
    n_cls = lax.axis_size("cls")
    pair = 2 if n_dom % 2 == 0 else 1
    z, x = lax.axis_index("dom"), lax.axis_index("cls")
    people = particles.shape[0]
    owned = CLASSES // (n_dom * n_cls)
    subs = n_dom // pair * owned
    parts = pair * n_cls
    label = classes.reshape(1, people)
    owner = label // owned
    z_of, x_of = owner // n_cls, owner % n_cls
    dest = (z_of % pair + pair - z % pair) % pair * n_cls + (x_of + n_cls - x) % n_cls
    index = z_of // pair * owned + label % owned
    meta = jnp.concatenate([dest, index, angles[None], counts[None], jnp.zeros((4, people), i32)], axis=0)
    mean_rows = people / parts
    most = min(CAP * subs, people + 15) // 16 * 16
    cap = min(most, -(-int(mean_rows + 3.2 * math.sqrt(mean_rows)) // 16) * 16)
    run = functools.partial(exchange, n_dom=n_dom, n_cls=n_cls, pair=pair)
    averages, gains, over = run(cap, particles, meta, z // pair)
    if cap == most:
        return averages, gains
    return lax.cond(
        over,
        lambda: run(most, particles, meta, z // pair)[:2],
        lambda: (averages, gains),
    )


def solution(mesh):
    in_specs = (
        P(("groups", "dom", "cls"), None, "coef"),
        P(("groups", "dom", "cls"), None),
        P(("groups", "dom", "cls")),
        P(("groups", "dom", "cls")),
    )
    out_specs = (P(("groups", "dom", "cls"), None, "coef"), P(("groups", "dom", "cls")))
    return jax.shard_map(shards, mesh=mesh, in_specs=in_specs, out_specs=out_specs, check_vma=False)
```

```python
import functools
import math

import jax
import jax.numpy as jnp
from jax import lax
from jax.experimental import pallas as pl
from jax.experimental.pallas import tpu as pltpu
from jax.sharding import PartitionSpec as P

NK = 80
NQ = 64
CLASSES = 256
CAP = 2
LANES = 128
BLOCK = 256
SHARES = (0.3, 0.3, 0.4)
PIN = 1
GATE = 0
HOLD = False
COST = 5
FLOWS = (3, 1, 2)
ROWS = 8
PARAMS = pltpu.CompilerParams(vmem_limit_bytes=20 << 20)
NT = (((1,), (1,)), ((), ()))
f32 = jnp.float32
bf16 = jnp.bfloat16
i32 = jnp.int32


def matmul(a, b, dims=(((1,), (0,)), ((), ()))):
    return lax.dot_general(a, b, dims, preferred_element_type=f32)


def split(value):
    high = value.astype(bf16)
    return high, (value - high.astype(f32)).astype(bf16)


def split3(value):
    high = value.astype(bf16)
    rest = value - high.astype(f32)
    mid = rest.astype(bf16)
    return high, mid, (rest - mid.astype(f32)).astype(bf16)


def place_of(slot, count):
    rows = lax.broadcasted_iota(i32, (count, slot.shape[1]), 0)
    return jnp.where(rows == slot, 1.0, 0.0).astype(bf16)


def pick_lanes(x_ref, lanes, start, width):
    return [x_ref[:, pl.ds(first + start, width)] for first in (0, lanes)]


def whole(value, by):
    return jnp.floor((value + 0.5) * (1.0 / by))


def pack_first(
    parts, cap, grid, width, x_ref, label_ref, angle_ref, count_ref, z_ref, column_ref, *refs
):
    out_refs, (held_ref, semaphore) = refs[:-2], refs[-2:]
    n_dom, n_cls, pair = grid
    copy = pltpu.make_async_copy(x_ref.at[:, :, pl.ds(0, width)], held_ref, semaphore)
    copy.start()
    slot_ref = out_refs[parts]
    people = label_ref.shape[1]
    owned = CLASSES // (n_dom * n_cls)
    label = label_ref[...].astype(f32)
    owner = whole(label, owned)
    z_of = whole(owner, n_cls)
    x_of = owner - n_cls * z_of
    group = whole(z_of, pair)
    depth = z_of - pair * group - lax.rem(z_ref[0, 0], pair).astype(f32)
    across = x_of - column_ref[0, 0].astype(f32)
    depth = jnp.where(depth < 0.0, depth + pair, depth)
    across = jnp.where(across < 0.0, across + n_cls, across)
    dest = (depth * n_cls + across).astype(i32)
    index = group * owned + label - owned * owner
    angle = angle_ref[...]
    chosen = jnp.where(lax.broadcasted_iota(i32, (16, people), 0) == dest, 1.0, 0.0)
    before = jnp.where(
        lax.broadcasted_iota(i32, (people, people), 0) < lax.broadcasted_iota(i32, (people, people), 1), 1.0, 0.0
    ).astype(bf16)
    ahead = matmul(chosen.astype(bf16), before)
    rank = jnp.sum(chosen * ahead, axis=0, keepdims=True).astype(i32)
    over = jnp.max(jnp.where(rank >= cap, 1.0, 0.0))
    slot = jnp.where(rank < cap, dest * cap + rank, -1)
    slot_ref[...] = jnp.broadcast_to(jnp.where(rank < cap, dest * LANES + rank, -1), slot_ref.shape)
    half = lax.shift_right_logical(angle, 1)
    rows = lax.broadcasted_iota(i32, (LANES, people), 0)
    details = jnp.where(rows == 0, index, 0.0)
    details = jnp.where(rows == 1, half.astype(f32), details)
    details = jnp.where(rows == 2, (angle - 2 * half).astype(f32), details)
    details = jnp.where(rows == 3, count_ref[...].astype(f32), details)
    details = details.astype(bf16)
    lane = lax.broadcasted_iota(i32, (cap, LANES), 1)
    copy.wait()
    real, imag = held_ref[:, 0, :], held_ref[:, 1, :]
    for part in range(parts):
        place = place_of(slot - part * cap, cap)
        out_refs[part][:, :width] = matmul(place, real).astype(bf16)
        out_refs[part][:, width : 2 * width] = matmul(place, imag).astype(bf16)
        block = jnp.where(lane == 4, over, matmul(place, details, NT))
        out_refs[part][:, 2 * width :] = block.astype(bf16)


def pack_next(parts, cap, lanes, start, width, slot_ref, x_ref, *out_refs):
    real, imag = pick_lanes(x_ref, lanes, start, width)
    slot = slot_ref[0:1]
    dest = lax.shift_right_arithmetic(slot, 7)
    slot = jnp.where(slot >= 0, dest * cap + (slot - dest * LANES), -1)
    for part in range(parts):
        place = place_of(slot - part * cap, cap)
        out_refs[part][:, :width] = matmul(place, real).astype(bf16)
        out_refs[part][:, width:] = matmul(place, imag).astype(bf16)


def align(parts, cap, subs, nfreq, first, freqs, start, *refs):
    width = freqs * NQ
    taken, refs = refs[:parts], refs[parts:]
    if first:
        core_ref, code_ref, sums_ref, high_ref, mid_ref, cos_ref, sin_ref, hot_ref, info_ref = refs
        core = core_ref[0, 0]
        columns = jnp.concatenate([ref[:, 2 * width :].astype(f32) for ref in taken], axis=0)
        details = columns.astype(bf16)
        angle = 2.0 * columns[:, 1:2] + columns[:, 2:3]
        rows = parts * cap
        lane = lax.broadcasted_iota(i32, (rows, cos_ref.shape[1]), 1)
        third = jnp.where(lane >= nfreq, 1, 0) + jnp.where(lane >= 2 * nfreq, 1, 0)
        frequency = (lane - third * nfreq + core * nfreq).astype(f32)
        turns = angle * frequency
        turns = turns - 360.0 * jnp.floor((turns + 0.5) * (1.0 / 360.0))
        theta = turns * (2.0 * math.pi / 360.0)
        for table, ref in ((jnp.cos(theta), cos_ref), (jnp.sin(theta), sin_ref)):
            high, mid, low = [piece.astype(f32) for piece in split3(table)]
            ref[...] = jnp.where(third == 0, high, jnp.where(third == 1, mid, low)).astype(bf16)
        pick = jnp.where(
            lax.broadcasted_iota(i32, (16, LANES), 0) == lax.broadcasted_iota(i32, (16, LANES), 1), 1.0, 0.0
        ).astype(bf16)
        flat = matmul(pick, details, NT)
        hot = jnp.where(lax.broadcasted_iota(i32, (subs, rows), 0) == flat[0:1].astype(i32), 1.0, 0.0)
        hot_ref[0] = hot.astype(bf16)
        weighted = hot * flat[3:4]
        hot_ref[1] = weighted.astype(bf16)
        totals = jnp.sum(weighted, axis=1, keepdims=True)
        over = jnp.max(flat[4:5])
        slot = lax.broadcasted_iota(i32, info_ref.shape, 1)
        info_ref[...] = jnp.where(slot == 1, totals, jnp.where(slot == 2, over, 0.0))
    else:
        cos_ref, sin_ref, hot_ref, code_ref, sums_ref, high_ref, mid_ref = refs
        info_ref = None
    lanes = cos_ref.shape[1]
    weights = hot_ref[1]
    cosines, sines = cos_ref[...], sin_ref[...]
    row = lax.broadcasted_iota(i32, (lanes, BLOCK), 0)
    row = row - jnp.where(row >= nfreq, nfreq, 0) - jnp.where(row >= 2 * nfreq, nfreq, 0)
    lane_freq = lax.shift_right_logical(lax.broadcasted_iota(i32, (lanes, BLOCK), 1), 6)
    inside = lax.broadcasted_iota(i32, (lanes, BLOCK), 0) < 3 * nfreq
    for block in range(width // BLOCK):
        at = pl.ds(block * BLOCK, BLOCK)
        at_im = pl.ds(width + block * BLOCK, BLOCK)
        spread = jnp.where(inside & (row == lane_freq + (start + block * (BLOCK // NQ))), 1.0, 0.0).astype(bf16)
        cosine, sine = matmul(cosines, spread), matmul(sines, spread)
        real = jnp.concatenate([ref[:, at].astype(f32) for ref in taken], axis=0)
        imag = jnp.concatenate([ref[:, at_im].astype(f32) for ref in taken], axis=0)
        for here, value in ((at, real * cosine - imag * sine), (at_im, real * sine + imag * cosine)):
            high, mid = split(value)
            high_ref[:, here] = high
            mid_ref[:, here] = mid
            sums_ref[:, here] = matmul(weights, high) + matmul(weights, mid)
    largest = jnp.maximum(jnp.max(jnp.abs(sums_ref[...]), axis=1, keepdims=True), 1e-30)
    level = jnp.ceil(jnp.log(largest) * (4.0 / math.log(2.0)) + 0.02)
    coded = jnp.floor(sums_ref[...] * jnp.exp2(15.0 - 0.25 * level) + 0.5)
    code_ref[:, : 2 * width] = coded.astype(i32).astype(jnp.int16)
    slot = lax.broadcasted_iota(i32, (subs, LANES), 1)
    extra = jnp.where(slot == 0, level, 0.0 if info_ref is None else info_ref[...])
    code_ref[:, 2 * width :] = extra.astype(i32).astype(jnp.int16)


def score(parts, cap, others, first, last, *refs):
    codes, refs = refs[:others], refs[others:]
    sums_ref, high_ref, mid_ref, hot_ref, info_ref, refs = *refs[:5], refs[5:]
    if first:
        mean_ref, total_ref, gain_ref = refs
        info = info_ref[...]
        for code_ref in codes:
            more = code_ref[:, sums_ref.shape[1] :].astype(i32).astype(f32)
            slot = lax.broadcasted_iota(i32, more.shape, 1)
            info = info + jnp.where(slot == 0, 0.0, more)
        total_ref[...] = info
        so_far = None
    else:
        so_far_ref, mean_ref, gain_ref = refs
        info = info_ref[...]
        so_far = so_far_ref[0:1]
    wide = sums_ref.shape[1]
    sums = sums_ref[...]
    for code_ref in codes:
        level = code_ref[:, wide:].astype(i32).astype(f32)[:, 0:1]
        sums = sums + code_ref[:, :wide].astype(i32).astype(f32) * jnp.exp2(0.25 * level - 15.0)
    mean = (sums / info[:, 1:2]).astype(bf16)
    mean_ref[...] = mean
    wide_mean = mean.astype(f32)
    norm = jnp.sum(wide_mean * wide_mean, axis=1, keepdims=True)
    product = matmul(mean, high_ref[...], NT) + matmul(mean, mid_ref[...], NT)
    gain = jnp.sum(hot_ref[0].astype(f32) * (2.0 * product - norm), axis=0, keepdims=True)
    if so_far is not None:
        gain = gain + so_far
    if last:
        gain_ref[...] = jnp.zeros(gain_ref.shape, f32)
        for part in range(parts):
            gain_ref[part : part + 1, :cap] = gain[:, part * cap : (part + 1) * cap]
    else:
        gain_ref[...] = jnp.broadcast_to(gain, gain_ref.shape)


def unpack(parts, slot_ref, *refs):
    returned, out_ref = refs[:parts], refs[parts]
    slot = slot_ref[0:1]
    total = jnp.zeros((8, slot.shape[1]), f32)
    for part in range(parts):
        place = place_of(slot - part * LANES, LANES)
        mine = jnp.broadcast_to(returned[part][part : part + 1], (8, LANES))
        for piece in split3(mine):
            total = total + matmul(piece, place)
    out_ref[...] = total[0:1] * (1.0 / math.sqrt(2.0 * NK * NQ))


def call(kernel, outs, *args, work=1, scalars=0, pin=False, far=0, scratch=()):
    shapes = [
        (pltpu.HBM if pin and math.prod(shape) > 1 << 15 else jax.ShapeDtypeStruct)(shape, dtype) for shape, dtype in outs
    ]
    specs = [pl.BlockSpec(memory_space=pl.ANY)] * far
    specs += [pl.BlockSpec(memory_space=pltpu.VMEM)] * (len(args) - scalars - far)
    specs += [pl.BlockSpec(memory_space=pltpu.SMEM)] * scalars
    places = [pl.BlockSpec(memory_space=pltpu.VMEM)] * len(outs)
    cost = pl.CostEstimate(flops=int(work * COST * 10**9), bytes_accessed=0, transcendentals=0) if COST else None
    return pl.pallas_call(
        kernel,
        in_specs=specs,
        out_specs=places,
        out_shape=shapes,
        scratch_shapes=scratch,
        cost_estimate=cost,
        compiler_params=PARAMS,
    )(*args)


def exchange(cap, particles, label, angles, counts, square, n_dom, n_cls, pair):
    people, _, width = particles.shape
    axes = ("dom", "cls")
    parts = pair * n_cls
    groups = n_dom // pair
    owned = CLASSES // (n_dom * n_cls)
    subs = groups * owned
    rows = parts * cap
    nfreq = width // NQ
    step = BLOCK // NQ
    sizes = [max(step, int(nfreq * share) // step * step) for share in SHARES[:-1]]
    sizes.append(nfreq - sum(sizes))
    devices = [(z, x) for z in range(n_dom) for x in range(n_cls)]

    def forward(part):
        dz, dx = divmod(part, n_cls)
        return [(z * n_cls + x, (z ^ dz) * n_cls + (x + dx) % n_cls) for z, x in devices]

    def across(turn):
        return [(z * n_cls + x, ((z // pair + turn) % groups * pair + z % pair) * n_cls + x) for z, x in devices]

    def deliver(packed):
        taken = {0: packed[0]}
        for part in FLOWS if parts == 4 else range(1, parts):
            taken[part] = lax.ppermute(packed[part], axes, forward(part))
        return [taken[part] for part in range(parts)]

    lanes = -(-3 * nfreq // LANES) * LANES
    starts = [sum(sizes[:i]) for i in range(len(sizes))]
    core = lax.axis_index("coef").reshape(1, 1).astype(i32)
    arrived = []
    rest = None
    for number, (start, freqs) in enumerate(zip(starts, sizes)):
        if number == 0:
            size = freqs * NQ
            *packed, slot = call(
                functools.partial(pack_first, parts, cap, (n_dom, n_cls, pair), size),
                [((cap, 2 * size + LANES), bf16)] * parts + [((8, people), i32)],
                particles,
                label,
                angles[None],
                counts[None],
                lax.axis_index("dom").reshape(1, 1).astype(i32),
                lax.axis_index("cls").reshape(1, 1).astype(i32),
                scalars=2,
                far=1,
                work=3,
                scratch=[pltpu.VMEM((people, 2, size), bf16), pltpu.SemaphoreType.DMA],
                pin=PIN >= 2,
            )
        else:
            if number == 1:
                rest = particles
                if HOLD:
                    rest, slot = lax.optimization_barrier((particles, slot))
                rest = rest.reshape(people, 2 * width)
            if GATE:
                slot, arrived[-1][GATE] = lax.optimization_barrier((slot, arrived[-1][GATE]))
            packed = call(
                functools.partial(pack_next, parts, cap, width, start * NQ, freqs * NQ),
                [((cap, 2 * freqs * NQ), bf16)] * parts,
                slot,
                rest,
                pin=PIN >= 2,
            )
        arrived.append(deliver(packed))
    aligned = []
    for number, (start, freqs) in enumerate(zip(starts, sizes)):
        wide = 2 * freqs * NQ
        kernel = functools.partial(align, parts, cap, subs, nfreq, number == 0, freqs, start)
        outs = [
            ((subs, wide + LANES), jnp.int16),
            ((subs, wide), f32),
            ((rows, wide), bf16),
            ((rows, wide), bf16),
        ]
        if number == 0:
            more = [((rows, lanes), bf16)] * 2 + [((2, subs, rows), bf16), ((subs, LANES), f32)]
            code, sums, high, mid, cosines, sines, hot, info = call(
                kernel, outs + more, *arrived[0], core, scalars=1, work=4, pin=PIN >= 1
            )
        else:
            code, sums, high, mid = call(
                kernel, outs, *arrived[number], cosines, sines, hot, work=3, pin=PIN >= 1
            )
        codes = [lax.ppermute(code, axes, across(turn)) for turn in range(1, groups)]
        aligned.append((codes, sums, high, mid))
    means = []
    gain = None
    for number, (codes, sums, high, mid) in enumerate(aligned):
        first, last = number == 0, number == len(sizes) - 1
        kernel = functools.partial(score, parts, cap, groups - 1, first, last)
        outs = [(sums.shape, bf16)]
        outs += [((subs, LANES), f32)] if first else []
        outs += [((-(-parts // 8) * 8, LANES), f32) if last else ((8, rows), f32)]
        args = [*codes, sums, high, mid, hot, info]
        if first:
            mean, *rest = call(kernel, outs, *args)
            info = rest[0]
            gain = rest[1]
        else:
            mean, gain = call(kernel, outs, *args, gain)
        means.append(mean)
    returned = [gain]
    for part in range(1, parts):
        returned.append(lax.ppermute(gain, axes, [(b, a) for a, b in forward(part)]))
    (gains,) = call(functools.partial(unpack, parts), [((1, people), f32)], slot, *returned)
    mine = [
        lax.dynamic_slice_in_dim(mean, square * owned, owned).reshape(owned, 2, -1) for mean in means
    ]
    averages = jnp.concatenate(mine, axis=2)
    return averages, gains, info[0, 2] > 0.0


def shards(particles, classes, angles, counts):
    n_dom = lax.axis_size("dom")
    n_cls = lax.axis_size("cls")
    pair = 2 if n_dom % 2 == 0 else 1
    z = lax.axis_index("dom")
    people = particles.shape[0]
    owned = CLASSES // (n_dom * n_cls)
    subs = n_dom // pair * owned
    parts = pair * n_cls
    label = classes.reshape(1, people)
    mean_rows = people / parts
    most = min(CAP * subs, people + ROWS - 1) // ROWS * ROWS
    cap = min(most, -(-int(mean_rows + 2.0 * math.sqrt(mean_rows)) // ROWS) * ROWS)
    run = functools.partial(exchange, n_dom=n_dom, n_cls=n_cls, pair=pair)
    averages, gains, over = run(cap, particles, label, angles, counts, z // pair)
    if cap < most:
        averages, gains = lax.cond(
            over,
            lambda: run(most, particles, label, angles, counts, z // pair)[:2],
            lambda: (averages, gains),
        )
    n_coef = lax.axis_size("coef")
    total = gains
    for turn in range(1, n_coef):
        total = total + lax.ppermute(gains, "coef", [(i, (i + turn) % n_coef) for i in range(n_coef)])
    return averages, total.reshape(people)


def solution(mesh):
    in_specs = (
        P(("groups", "dom", "cls"), None, "coef"),
        P(("groups", "dom", "cls"), None),
        P(("groups", "dom", "cls")),
        P(("groups", "dom", "cls")),
    )
    out_specs = (P(("groups", "dom", "cls"), None, "coef"), P(("groups", "dom", "cls")))
    return jax.shard_map(shards, mesh=mesh, in_specs=in_specs, out_specs=out_specs, check_vma=False)
```

```python
import functools
import math

import jax
import jax.numpy as jnp
from jax import lax
from jax.experimental import pallas as pl
from jax.experimental.pallas import tpu as pltpu
from jax.sharding import PartitionSpec as P

NK = 80
NQ = 64
CLASSES = 256
CAP = 2
LANES = 128
BLOCK = 256
SHARES = (0.3, 0.4, 0.3)
PIN = (0, 1, 2, 3)
KEEP = (0,)
COST = 5
FLOWS = (3, 1, 2)
ROWS = 8
PARAMS = pltpu.CompilerParams(vmem_limit_bytes=20 << 20)
NT = (((1,), (1,)), ((), ()))
f32 = jnp.float32
bf16 = jnp.bfloat16
i32 = jnp.int32


def matmul(a, b, dims=(((1,), (0,)), ((), ()))):
    return lax.dot_general(a, b, dims, preferred_element_type=f32)


def split(value):
    high = value.astype(bf16)
    return high, (value - high.astype(f32)).astype(bf16)


def split3(value):
    high = value.astype(bf16)
    rest = value - high.astype(f32)
    mid = rest.astype(bf16)
    return high, mid, (rest - mid.astype(f32)).astype(bf16)


def place_of(slot, count):
    rows = lax.broadcasted_iota(i32, (count, slot.shape[1]), 0)
    return jnp.where(rows == slot, 1.0, 0.0).astype(bf16)


def pick_lanes(x_ref, lanes, start, width):
    return [x_ref[:, pl.ds(first + start, width)] for first in (0, lanes)]


def whole(value, by):
    return jnp.floor((value + 0.5) * (1.0 / by))


def pack_first(
    parts, cap, grid, lanes, width, x_ref, label_ref, angle_ref, count_ref, z_ref, column_ref, *out_refs
):
    n_dom, n_cls, pair = grid
    slot_ref = out_refs[parts]
    people = label_ref.shape[1]
    owned = CLASSES // (n_dom * n_cls)
    label = label_ref[...].astype(f32)
    owner = whole(label, owned)
    z_of = whole(owner, n_cls)
    x_of = owner - n_cls * z_of
    group = whole(z_of, pair)
    depth = z_of - pair * group - lax.rem(z_ref[0, 0], pair).astype(f32)
    across = x_of - column_ref[0, 0].astype(f32)
    depth = jnp.where(depth < 0.0, depth + pair, depth)
    across = jnp.where(across < 0.0, across + n_cls, across)
    dest = (depth * n_cls + across).astype(i32)
    index = group * owned + label - owned * owner
    angle = angle_ref[...]
    chosen = jnp.where(lax.broadcasted_iota(i32, (16, people), 0) == dest, 1.0, 0.0)
    before = jnp.where(
        lax.broadcasted_iota(i32, (people, people), 0) < lax.broadcasted_iota(i32, (people, people), 1), 1.0, 0.0
    ).astype(bf16)
    ahead = matmul(chosen.astype(bf16), before)
    rank = jnp.sum(chosen * ahead, axis=0, keepdims=True).astype(i32)
    over = jnp.max(jnp.where(rank >= cap, 1.0, 0.0))
    slot = jnp.where(rank < cap, dest * cap + rank, -1)
    slot_ref[...] = jnp.broadcast_to(jnp.where(rank < cap, dest * LANES + rank, -1), slot_ref.shape)
    half = lax.shift_right_logical(angle, 1)
    rows = lax.broadcasted_iota(i32, (LANES, people), 0)
    details = jnp.where(rows == 0, index, 0.0)
    details = jnp.where(rows == 1, half.astype(f32), details)
    details = jnp.where(rows == 2, (angle - 2 * half).astype(f32), details)
    details = jnp.where(rows == 3, count_ref[...].astype(f32), details)
    details = details.astype(bf16)
    lane = lax.broadcasted_iota(i32, (cap, LANES), 1)
    real, imag = pick_lanes(x_ref, lanes, 0, width)
    for part in range(parts):
        place = place_of(slot - part * cap, cap)
        out_refs[part][:, :width] = matmul(place, real).astype(bf16)
        out_refs[part][:, width : 2 * width] = matmul(place, imag).astype(bf16)
        block = jnp.where(lane == 4, over, matmul(place, details, NT))
        out_refs[part][:, 2 * width :] = block.astype(bf16)


def pack_next(parts, cap, lanes, start, width, slot_ref, x_ref, *out_refs):
    real, imag = pick_lanes(x_ref, lanes, start, width)
    slot = slot_ref[0:1]
    dest = lax.shift_right_arithmetic(slot, 7)
    slot = jnp.where(slot >= 0, dest * cap + (slot - dest * LANES), -1)
    for part in range(parts):
        place = place_of(slot - part * cap, cap)
        out_refs[part][:, :width] = matmul(place, real).astype(bf16)
        out_refs[part][:, width:] = matmul(place, imag).astype(bf16)


def align(parts, cap, subs, nfreq, first, freqs, start, *refs):
    width = freqs * NQ
    taken, refs = refs[:parts], refs[parts:]
    if first:
        core_ref, code_ref, sums_ref, high_ref, mid_ref, cos_ref, sin_ref, hot_ref, info_ref = refs
        core = core_ref[0, 0]
        columns = jnp.concatenate([ref[:, 2 * width :].astype(f32) for ref in taken], axis=0)
        details = columns.astype(bf16)
        angle = 2.0 * columns[:, 1:2] + columns[:, 2:3]
        rows = parts * cap
        lane = lax.broadcasted_iota(i32, (rows, cos_ref.shape[1]), 1)
        third = jnp.where(lane >= nfreq, 1, 0) + jnp.where(lane >= 2 * nfreq, 1, 0)
        frequency = (lane - third * nfreq + core * nfreq).astype(f32)
        turns = angle * frequency
        turns = turns - 360.0 * jnp.floor((turns + 0.5) * (1.0 / 360.0))
        theta = turns * (2.0 * math.pi / 360.0)
        for table, ref in ((jnp.cos(theta), cos_ref), (jnp.sin(theta), sin_ref)):
            high, mid, low = [piece.astype(f32) for piece in split3(table)]
            ref[...] = jnp.where(third == 0, high, jnp.where(third == 1, mid, low)).astype(bf16)
        pick = jnp.where(
            lax.broadcasted_iota(i32, (16, LANES), 0) == lax.broadcasted_iota(i32, (16, LANES), 1), 1.0, 0.0
        ).astype(bf16)
        flat = matmul(pick, details, NT)
        hot = jnp.where(lax.broadcasted_iota(i32, (subs, rows), 0) == flat[0:1].astype(i32), 1.0, 0.0)
        hot_ref[0] = hot.astype(bf16)
        weighted = hot * flat[3:4]
        hot_ref[1] = weighted.astype(bf16)
        totals = jnp.sum(weighted, axis=1, keepdims=True)
        over = jnp.max(flat[4:5])
        slot = lax.broadcasted_iota(i32, info_ref.shape, 1)
        info_ref[...] = jnp.where(slot == 1, totals, jnp.where(slot == 2, over, 0.0))
    else:
        cos_ref, sin_ref, hot_ref, code_ref, sums_ref, high_ref, mid_ref = refs
        info_ref = None
    lanes = cos_ref.shape[1]
    weights = hot_ref[1]
    cosines, sines = cos_ref[...], sin_ref[...]
    row = lax.broadcasted_iota(i32, (lanes, BLOCK), 0)
    row = row - jnp.where(row >= nfreq, nfreq, 0) - jnp.where(row >= 2 * nfreq, nfreq, 0)
    lane_freq = lax.shift_right_logical(lax.broadcasted_iota(i32, (lanes, BLOCK), 1), 6)
    inside = lax.broadcasted_iota(i32, (lanes, BLOCK), 0) < 3 * nfreq
    for block in range(width // BLOCK):
        at = pl.ds(block * BLOCK, BLOCK)
        at_im = pl.ds(width + block * BLOCK, BLOCK)
        spread = jnp.where(inside & (row == lane_freq + (start + block * (BLOCK // NQ))), 1.0, 0.0).astype(bf16)
        cosine, sine = matmul(cosines, spread), matmul(sines, spread)
        real = jnp.concatenate([ref[:, at].astype(f32) for ref in taken], axis=0)
        imag = jnp.concatenate([ref[:, at_im].astype(f32) for ref in taken], axis=0)
        for here, value in ((at, real * cosine - imag * sine), (at_im, real * sine + imag * cosine)):
            high, mid = split(value)
            high_ref[:, here] = high
            mid_ref[:, here] = mid
            sums_ref[:, here] = matmul(weights, high) + matmul(weights, mid)
    largest = jnp.maximum(jnp.max(jnp.abs(sums_ref[...]), axis=1, keepdims=True), 1e-30)
    level = jnp.ceil(jnp.log(largest) * (4.0 / math.log(2.0)) + 0.02)
    coded = jnp.floor(sums_ref[...] * jnp.exp2(15.0 - 0.25 * level) + 0.5)
    code_ref[:, : 2 * width] = coded.astype(i32).astype(jnp.int16)
    slot = lax.broadcasted_iota(i32, (subs, LANES), 1)
    extra = jnp.where(slot == 0, level, 0.0 if info_ref is None else info_ref[...])
    code_ref[:, 2 * width :] = extra.astype(i32).astype(jnp.int16)


def score(parts, cap, others, first, last, *refs):
    codes, refs = refs[:others], refs[others:]
    sums_ref, high_ref, mid_ref, hot_ref, info_ref, refs = *refs[:5], refs[5:]
    if first:
        mean_ref, total_ref, gain_ref = refs
        info = info_ref[...]
        for code_ref in codes:
            more = code_ref[:, sums_ref.shape[1] :].astype(i32).astype(f32)
            slot = lax.broadcasted_iota(i32, more.shape, 1)
            info = info + jnp.where(slot == 0, 0.0, more)
        total_ref[...] = info
        so_far = None
    else:
        so_far_ref, mean_ref, gain_ref = refs
        info = info_ref[...]
        so_far = so_far_ref[0:1]
    wide = sums_ref.shape[1]
    sums = sums_ref[...]
    for code_ref in codes:
        level = code_ref[:, wide:].astype(i32).astype(f32)[:, 0:1]
        sums = sums + code_ref[:, :wide].astype(i32).astype(f32) * jnp.exp2(0.25 * level - 15.0)
    mean = (sums / info[:, 1:2]).astype(bf16)
    mean_ref[...] = mean
    wide_mean = mean.astype(f32)
    norm = jnp.sum(wide_mean * wide_mean, axis=1, keepdims=True)
    product = matmul(mean, high_ref[...], NT) + matmul(mean, mid_ref[...], NT)
    gain = jnp.sum(hot_ref[0].astype(f32) * (2.0 * product - norm), axis=0, keepdims=True)
    if so_far is not None:
        gain = gain + so_far
    if last:
        gain_ref[...] = jnp.zeros(gain_ref.shape, f32)
        for part in range(parts):
            gain_ref[part : part + 1, :cap] = gain[:, part * cap : (part + 1) * cap]
    else:
        gain_ref[...] = jnp.broadcast_to(gain, gain_ref.shape)


def unpack(parts, slot_ref, *refs):
    returned, out_ref = refs[:parts], refs[parts]
    slot = slot_ref[0:1]
    total = jnp.zeros((8, slot.shape[1]), f32)
    for part in range(parts):
        place = place_of(slot - part * LANES, LANES)
        mine = jnp.broadcast_to(returned[part][part : part + 1], (8, LANES))
        for piece in split3(mine):
            total = total + matmul(piece, place)
    out_ref[...] = total[0:1] * (1.0 / math.sqrt(2.0 * NK * NQ))


def call(kernel, outs, *args, work=1, scalars=0, pin=()):
    shapes = [
        (pltpu.HBM if number in pin else jax.ShapeDtypeStruct)(shape, dtype)
        for number, (shape, dtype) in enumerate(outs)
    ]
    specs = [pl.BlockSpec(memory_space=pltpu.VMEM)] * (len(args) - scalars)
    specs += [pl.BlockSpec(memory_space=pltpu.SMEM)] * scalars
    places = [pl.BlockSpec(memory_space=pltpu.VMEM)] * len(outs)
    cost = pl.CostEstimate(flops=int(work * COST * 10**9), bytes_accessed=0, transcendentals=0) if COST else None
    return pl.pallas_call(
        kernel,
        in_specs=specs,
        out_specs=places,
        out_shape=shapes,
        cost_estimate=cost,
        compiler_params=PARAMS,
    )(*args)


def exchange(cap, particles, label, angles, counts, square, n_dom, n_cls, pair):
    people, _, width = particles.shape
    axes = ("dom", "cls")
    parts = pair * n_cls
    groups = n_dom // pair
    owned = CLASSES // (n_dom * n_cls)
    subs = groups * owned
    rows = parts * cap
    nfreq = width // NQ
    step = BLOCK // NQ
    sizes = [max(step, int(nfreq * share) // step * step) for share in SHARES[:-1]]
    sizes.append(nfreq - sum(sizes))
    devices = [(z, x) for z in range(n_dom) for x in range(n_cls)]

    def forward(part):
        dz, dx = divmod(part, n_cls)
        return [(z * n_cls + x, (z ^ dz) * n_cls + (x + dx) % n_cls) for z, x in devices]

    def across(turn):
        return [(z * n_cls + x, ((z // pair + turn) % groups * pair + z % pair) * n_cls + x) for z, x in devices]

    def deliver(packed):
        taken = {0: packed[0]}
        for part in FLOWS if parts == 4 else range(1, parts):
            taken[part] = lax.ppermute(packed[part], axes, forward(part))
        return [taken[part] for part in range(parts)]

    lanes = -(-3 * nfreq // LANES) * LANES
    starts = [sum(sizes[:i]) for i in range(len(sizes))]
    core = lax.axis_index("coef").reshape(1, 1).astype(i32)
    arrived, codes, kept, tables = [], [], [], []
    rest = particles.reshape(people, 2 * width)
    slot = None

    def turn(number):
        start, freqs = starts[number], sizes[number]
        wide = 2 * freqs * NQ
        kernel = functools.partial(align, parts, cap, subs, nfreq, number == 0, freqs, start)
        outs = [((subs, wide + LANES), jnp.int16), ((subs, wide), f32), ((rows, wide), bf16), ((rows, wide), bf16)]
        if number == 0:
            outs += [((rows, lanes), bf16)] * 2 + [((2, subs, rows), bf16), ((subs, LANES), f32)]
            code, *held = call(kernel, outs, *arrived[0], core, scalars=1, work=4, pin=(*PIN, 6))
            tables.extend(held[3:])
        else:
            code, *held = call(kernel, outs, *arrived[number], *tables[:3], work=3, pin=PIN)
        codes.append(code)
        kept.append(held[:3])

    for number, (start, freqs) in enumerate(zip(starts, sizes)):
        if number == 0:
            size = freqs * NQ
            *packed, slot = call(
                functools.partial(pack_first, parts, cap, (n_dom, n_cls, pair), width, size),
                [((cap, 2 * size + LANES), bf16)] * parts + [((8, people), i32)],
                rest,
                label,
                angles[None],
                counts[None],
                lax.axis_index("dom").reshape(1, 1).astype(i32),
                lax.axis_index("cls").reshape(1, 1).astype(i32),
                scalars=2,
                work=3,
                pin=KEEP,
            )
        else:
            if number >= 2:
                slot, codes[-1] = lax.optimization_barrier((slot, codes[-1]))
            packed = call(
                functools.partial(pack_next, parts, cap, width, start * NQ, freqs * NQ),
                [((cap, 2 * freqs * NQ), bf16)] * parts,
                slot,
                rest,
                pin=KEEP,
            )
        arrived.append(deliver(packed))
        if number >= 1:
            turn(number - 1)
    turn(len(sizes) - 1)
    aligned = [
        ([lax.ppermute(code, axes, across(step)) for step in range(1, groups)], *rows_of)
        for code, rows_of in zip(codes, kept)
    ]
    means = []
    gain = None
    hot, info = tables[2:]
    for number, (codes, sums, high, mid) in enumerate(aligned):
        first, last = number == 0, number == len(sizes) - 1
        kernel = functools.partial(score, parts, cap, groups - 1, first, last)
        outs = [(sums.shape, bf16)]
        outs += [((subs, LANES), f32)] if first else []
        outs += [((-(-parts // 8) * 8, LANES), f32) if last else ((8, rows), f32)]
        args = [*codes, sums, high, mid, hot, info]
        if first:
            mean, *rest = call(kernel, outs, *args)
            info = rest[0]
            gain = rest[1]
        else:
            mean, gain = call(kernel, outs, *args, gain)
        means.append(mean)
    returned = [gain]
    for part in range(1, parts):
        returned.append(lax.ppermute(gain, axes, [(b, a) for a, b in forward(part)]))
    (gains,) = call(functools.partial(unpack, parts), [((1, people), f32)], slot, *returned)
    mine = [
        lax.dynamic_slice_in_dim(mean, square * owned, owned).reshape(owned, 2, -1) for mean in means
    ]
    averages = jnp.concatenate(mine, axis=2)
    return averages, gains, info[0, 2] > 0.0


def shards(particles, classes, angles, counts):
    n_dom = lax.axis_size("dom")
    n_cls = lax.axis_size("cls")
    pair = 2 if n_dom % 2 == 0 else 1
    z = lax.axis_index("dom")
    people = particles.shape[0]
    owned = CLASSES // (n_dom * n_cls)
    subs = n_dom // pair * owned
    parts = pair * n_cls
    label = classes.reshape(1, people)
    mean_rows = people / parts
    most = min(CAP * subs, people + ROWS - 1) // ROWS * ROWS
    cap = min(most, -(-int(mean_rows + 2.0 * math.sqrt(mean_rows)) // ROWS) * ROWS)
    run = functools.partial(exchange, n_dom=n_dom, n_cls=n_cls, pair=pair)
    averages, gains, over = run(cap, particles, label, angles, counts, z // pair)
    if cap < most:
        averages, gains = lax.cond(
            over,
            lambda: run(most, particles, label, angles, counts, z // pair)[:2],
            lambda: (averages, gains),
        )
    n_coef = lax.axis_size("coef")
    total = gains
    for turn in range(1, n_coef):
        total = total + lax.ppermute(gains, "coef", [(i, (i + turn) % n_coef) for i in range(n_coef)])
    return averages, total.reshape(people)


def solution(mesh):
    in_specs = (
        P(("groups", "dom", "cls"), None, "coef"),
        P(("groups", "dom", "cls"), None),
        P(("groups", "dom", "cls")),
        P(("groups", "dom", "cls")),
    )
    out_specs = (P(("groups", "dom", "cls"), None, "coef"), P(("groups", "dom", "cls")))
    return jax.shard_map(shards, mesh=mesh, in_specs=in_specs, out_specs=out_specs, check_vma=False)
```

```python
import functools
import math

import jax
import jax.numpy as jnp
from jax import lax
from jax.experimental import pallas as pl
from jax.experimental.pallas import tpu as pltpu
from jax.sharding import PartitionSpec as P

NK = 80
NQ = 64
CLASSES = 256
CAP = 2
LANES = 128
BLOCK = 256
SHARES = (0.3, 0.4, 0.3)
PIN = (1, 2, 3)
KEEP = (0,)
COST = 5
FLOWS = (3, 1, 2)
ROWS = 8
PARAMS = pltpu.CompilerParams(vmem_limit_bytes=20 << 20)
NT = (((1,), (1,)), ((), ()))
f32 = jnp.float32
bf16 = jnp.bfloat16
i32 = jnp.int32


def matmul(a, b, dims=(((1,), (0,)), ((), ()))):
    return lax.dot_general(a, b, dims, preferred_element_type=f32)


def split(value):
    high = value.astype(bf16)
    return high, (value - high.astype(f32)).astype(bf16)


def split3(value):
    high = value.astype(bf16)
    rest = value - high.astype(f32)
    mid = rest.astype(bf16)
    return high, mid, (rest - mid.astype(f32)).astype(bf16)


def place_of(slot, count):
    rows = lax.broadcasted_iota(i32, (count, slot.shape[1]), 0)
    return jnp.where(rows == slot, 1.0, 0.0).astype(bf16)


def pick_lanes(x_ref, lanes, start, width):
    return [x_ref[:, pl.ds(first + start, width)] for first in (0, lanes)]


def whole(value, by):
    return jnp.floor((value + 0.5) * (1.0 / by))


def pack_first(
    parts, cap, grid, lanes, width, x_ref, label_ref, angle_ref, count_ref, z_ref, column_ref, *out_refs
):
    n_dom, n_cls, pair = grid
    slot_ref = out_refs[parts]
    people = label_ref.shape[1]
    owned = CLASSES // (n_dom * n_cls)
    label = label_ref[...].astype(f32)
    owner = whole(label, owned)
    z_of = whole(owner, n_cls)
    x_of = owner - n_cls * z_of
    group = whole(z_of, pair)
    depth = z_of - pair * group - lax.rem(z_ref[0, 0], pair).astype(f32)
    across = x_of - column_ref[0, 0].astype(f32)
    depth = jnp.where(depth < 0.0, depth + pair, depth)
    across = jnp.where(across < 0.0, across + n_cls, across)
    dest = (depth * n_cls + across).astype(i32)
    index = group * owned + label - owned * owner
    angle = angle_ref[...]
    chosen = jnp.where(lax.broadcasted_iota(i32, (16, people), 0) == dest, 1.0, 0.0)
    before = jnp.where(
        lax.broadcasted_iota(i32, (people, people), 0) < lax.broadcasted_iota(i32, (people, people), 1), 1.0, 0.0
    ).astype(bf16)
    ahead = matmul(chosen.astype(bf16), before)
    rank = jnp.sum(chosen * ahead, axis=0, keepdims=True).astype(i32)
    over = jnp.max(jnp.where(rank >= cap, 1.0, 0.0))
    slot = jnp.where(rank < cap, dest * cap + rank, -1)
    slot_ref[...] = jnp.broadcast_to(jnp.where(rank < cap, dest * LANES + rank, -1), slot_ref.shape)
    half = lax.shift_right_logical(angle, 1)
    rows = lax.broadcasted_iota(i32, (LANES, people), 0)
    details = jnp.where(rows == 0, index, 0.0)
    details = jnp.where(rows == 1, half.astype(f32), details)
    details = jnp.where(rows == 2, (angle - 2 * half).astype(f32), details)
    details = jnp.where(rows == 3, count_ref[...].astype(f32), details)
    details = details.astype(bf16)
    lane = lax.broadcasted_iota(i32, (cap, LANES), 1)
    real, imag = pick_lanes(x_ref, lanes, 0, width)
    for part in range(parts):
        place = place_of(slot - part * cap, cap)
        out_refs[part][:, :width] = matmul(place, real).astype(bf16)
        out_refs[part][:, width : 2 * width] = matmul(place, imag).astype(bf16)
        block = jnp.where(lane == 4, over, matmul(place, details, NT))
        out_refs[part][:, 2 * width :] = block.astype(bf16)


def pack_next(parts, cap, lanes, start, width, slot_ref, x_ref, *out_refs):
    real, imag = pick_lanes(x_ref, lanes, start, width)
    slot = slot_ref[0:1]
    dest = lax.shift_right_arithmetic(slot, 7)
    slot = jnp.where(slot >= 0, dest * cap + (slot - dest * LANES), -1)
    for part in range(parts):
        place = place_of(slot - part * cap, cap)
        out_refs[part][:, :width] = matmul(place, real).astype(bf16)
        out_refs[part][:, width:] = matmul(place, imag).astype(bf16)


def align(parts, cap, subs, nfreq, first, freqs, start, *refs):
    width = freqs * NQ
    taken, refs = refs[:parts], refs[parts:]
    if first:
        core_ref, code_ref, sums_ref, high_ref, mid_ref, cos_ref, sin_ref, hot_ref, info_ref = refs
        core = core_ref[0, 0]
        columns = jnp.concatenate([ref[:, 2 * width :].astype(f32) for ref in taken], axis=0)
        details = columns.astype(bf16)
        angle = 2.0 * columns[:, 1:2] + columns[:, 2:3]
        rows = parts * cap
        lane = lax.broadcasted_iota(i32, (rows, cos_ref.shape[1]), 1)
        third = jnp.where(lane >= nfreq, 1, 0) + jnp.where(lane >= 2 * nfreq, 1, 0)
        frequency = (lane - third * nfreq + core * nfreq).astype(f32)
        turns = angle * frequency
        turns = turns - 360.0 * jnp.floor((turns + 0.5) * (1.0 / 360.0))
        theta = turns * (2.0 * math.pi / 360.0)
        for table, ref in ((jnp.cos(theta), cos_ref), (jnp.sin(theta), sin_ref)):
            high, mid, low = [piece.astype(f32) for piece in split3(table)]
            ref[...] = jnp.where(third == 0, high, jnp.where(third == 1, mid, low)).astype(bf16)
        pick = jnp.where(
            lax.broadcasted_iota(i32, (16, LANES), 0) == lax.broadcasted_iota(i32, (16, LANES), 1), 1.0, 0.0
        ).astype(bf16)
        flat = matmul(pick, details, NT)
        hot = jnp.where(lax.broadcasted_iota(i32, (subs, rows), 0) == flat[0:1].astype(i32), 1.0, 0.0)
        hot_ref[0] = hot.astype(bf16)
        weighted = hot * flat[3:4]
        hot_ref[1] = weighted.astype(bf16)
        totals = jnp.sum(weighted, axis=1, keepdims=True)
        over = jnp.max(flat[4:5])
        slot = lax.broadcasted_iota(i32, info_ref.shape, 1)
        info_ref[...] = jnp.where(slot == 1, totals, jnp.where(slot == 2, over, 0.0))
    else:
        cos_ref, sin_ref, hot_ref, code_ref, sums_ref, high_ref, mid_ref = refs
        info_ref = None
    lanes = cos_ref.shape[1]
    weights = hot_ref[1]
    cosines, sines = cos_ref[...], sin_ref[...]
    row = lax.broadcasted_iota(i32, (lanes, BLOCK), 0)
    row = row - jnp.where(row >= nfreq, nfreq, 0) - jnp.where(row >= 2 * nfreq, nfreq, 0)
    lane_freq = lax.shift_right_logical(lax.broadcasted_iota(i32, (lanes, BLOCK), 1), 6)
    inside = lax.broadcasted_iota(i32, (lanes, BLOCK), 0) < 3 * nfreq
    for block in range(width // BLOCK):
        at = pl.ds(block * BLOCK, BLOCK)
        at_im = pl.ds(width + block * BLOCK, BLOCK)
        spread = jnp.where(inside & (row == lane_freq + (start + block * (BLOCK // NQ))), 1.0, 0.0).astype(bf16)
        cosine, sine = matmul(cosines, spread), matmul(sines, spread)
        real = jnp.concatenate([ref[:, at].astype(f32) for ref in taken], axis=0)
        imag = jnp.concatenate([ref[:, at_im].astype(f32) for ref in taken], axis=0)
        for here, value in ((at, real * cosine - imag * sine), (at_im, real * sine + imag * cosine)):
            high, mid = split(value)
            high_ref[:, here] = high
            mid_ref[:, here] = mid
            sums_ref[:, here] = matmul(weights, high) + matmul(weights, mid)
    largest = jnp.maximum(jnp.max(jnp.abs(sums_ref[...]), axis=1, keepdims=True), 1e-30)
    level = jnp.ceil(jnp.log(largest) * (4.0 / math.log(2.0)) + 0.02)
    coded = jnp.floor(sums_ref[...] * jnp.exp2(15.0 - 0.25 * level) + 0.5)
    code_ref[:, : 2 * width] = coded.astype(i32).astype(jnp.int16)
    slot = lax.broadcasted_iota(i32, (subs, LANES), 1)
    extra = jnp.where(slot == 0, level, 0.0 if info_ref is None else info_ref[...])
    code_ref[:, 2 * width :] = extra.astype(i32).astype(jnp.int16)


def score(parts, cap, others, first, last, *refs):
    codes, refs = refs[:others], refs[others:]
    sums_ref, high_ref, mid_ref, hot_ref, info_ref, refs = *refs[:5], refs[5:]
    if first:
        mean_ref, total_ref, gain_ref = refs
        info = info_ref[...]
        for code_ref in codes:
            more = code_ref[:, sums_ref.shape[1] :].astype(i32).astype(f32)
            slot = lax.broadcasted_iota(i32, more.shape, 1)
            info = info + jnp.where(slot == 0, 0.0, more)
        total_ref[...] = info
        so_far = None
    else:
        so_far_ref, mean_ref, gain_ref = refs
        info = info_ref[...]
        so_far = so_far_ref[0:1]
    wide = sums_ref.shape[1]
    sums = sums_ref[...]
    for code_ref in codes:
        level = code_ref[:, wide:].astype(i32).astype(f32)[:, 0:1]
        sums = sums + code_ref[:, :wide].astype(i32).astype(f32) * jnp.exp2(0.25 * level - 15.0)
    mean = (sums / info[:, 1:2]).astype(bf16)
    mean_ref[...] = mean
    wide_mean = mean.astype(f32)
    norm = jnp.sum(wide_mean * wide_mean, axis=1, keepdims=True)
    product = matmul(mean, high_ref[...], NT) + matmul(mean, mid_ref[...], NT)
    gain = jnp.sum(hot_ref[0].astype(f32) * (2.0 * product - norm), axis=0, keepdims=True)
    if so_far is not None:
        gain = gain + so_far
    if last:
        gain_ref[...] = jnp.zeros(gain_ref.shape, f32)
        for part in range(parts):
            gain_ref[part : part + 1, :cap] = gain[:, part * cap : (part + 1) * cap]
    else:
        gain_ref[...] = jnp.broadcast_to(gain, gain_ref.shape)


def unpack(parts, slot_ref, *refs):
    returned, out_ref = refs[:parts], refs[parts]
    slot = slot_ref[0:1]
    total = jnp.zeros((8, slot.shape[1]), f32)
    for part in range(parts):
        place = place_of(slot - part * LANES, LANES)
        mine = jnp.broadcast_to(returned[part][part : part + 1], (8, LANES))
        for piece in split3(mine):
            total = total + matmul(piece, place)
    out_ref[...] = total[0:1] * (1.0 / math.sqrt(2.0 * NK * NQ))


def call(kernel, outs, *args, work=1, scalars=0, pin=()):
    shapes = [
        (pltpu.HBM if number in pin else jax.ShapeDtypeStruct)(shape, dtype)
        for number, (shape, dtype) in enumerate(outs)
    ]
    specs = [pl.BlockSpec(memory_space=pltpu.VMEM)] * (len(args) - scalars)
    specs += [pl.BlockSpec(memory_space=pltpu.SMEM)] * scalars
    places = [pl.BlockSpec(memory_space=pltpu.VMEM)] * len(outs)
    cost = pl.CostEstimate(flops=int(work * COST * 10**9), bytes_accessed=0, transcendentals=0) if COST else None
    return pl.pallas_call(
        kernel,
        in_specs=specs,
        out_specs=places,
        out_shape=shapes,
        cost_estimate=cost,
        compiler_params=PARAMS,
    )(*args)


def exchange(cap, particles, label, angles, counts, square, n_dom, n_cls, pair):
    people, _, width = particles.shape
    axes = ("dom", "cls")
    parts = pair * n_cls
    groups = n_dom // pair
    owned = CLASSES // (n_dom * n_cls)
    subs = groups * owned
    rows = parts * cap
    nfreq = width // NQ
    step = BLOCK // NQ
    sizes = [max(step, int(nfreq * share) // step * step) for share in SHARES[:-1]]
    sizes.append(nfreq - sum(sizes))
    devices = [(z, x) for z in range(n_dom) for x in range(n_cls)]

    def forward(part):
        dz, dx = divmod(part, n_cls)
        return [(z * n_cls + x, (z ^ dz) * n_cls + (x + dx) % n_cls) for z, x in devices]

    def across(turn):
        return [(z * n_cls + x, ((z // pair + turn) % groups * pair + z % pair) * n_cls + x) for z, x in devices]

    def deliver(packed):
        taken = {0: packed[0]}
        for part in FLOWS if parts == 4 else range(1, parts):
            taken[part] = lax.ppermute(packed[part], axes, forward(part))
        return [taken[part] for part in range(parts)]

    lanes = -(-3 * nfreq // LANES) * LANES
    starts = [sum(sizes[:i]) for i in range(len(sizes))]
    core = lax.axis_index("coef").reshape(1, 1).astype(i32)
    arrived, codes, kept, tables = [], [], [], []
    rest = particles.reshape(people, 2 * width)
    slot = None

    def turn(number):
        start, freqs = starts[number], sizes[number]
        wide = 2 * freqs * NQ
        kernel = functools.partial(align, parts, cap, subs, nfreq, number == 0, freqs, start)
        outs = [((subs, wide + LANES), jnp.int16), ((subs, wide), f32), ((rows, wide), bf16), ((rows, wide), bf16)]
        if number == 0:
            outs += [((rows, lanes), bf16)] * 2 + [((2, subs, rows), bf16), ((subs, LANES), f32)]
            code, *held = call(kernel, outs, *arrived[0], core, scalars=1, work=4, pin=(*PIN, 6))
            tables.extend(held[3:])
        else:
            code, *held = call(kernel, outs, *arrived[number], *tables[:3], work=3, pin=PIN)
        codes.append(code)
        kept.append(held[:3])

    for number, (start, freqs) in enumerate(zip(starts, sizes)):
        if number == 0:
            size = freqs * NQ
            *packed, slot = call(
                functools.partial(pack_first, parts, cap, (n_dom, n_cls, pair), width, size),
                [((cap, 2 * size + LANES), bf16)] * parts + [((8, people), i32)],
                rest,
                label,
                angles[None],
                counts[None],
                lax.axis_index("dom").reshape(1, 1).astype(i32),
                lax.axis_index("cls").reshape(1, 1).astype(i32),
                scalars=2,
                work=3,
                pin=KEEP,
            )
        else:
            if number >= 2:
                slot, codes[-1] = lax.optimization_barrier((slot, codes[-1]))
            packed = call(
                functools.partial(pack_next, parts, cap, width, start * NQ, freqs * NQ),
                [((cap, 2 * freqs * NQ), bf16)] * parts,
                slot,
                rest,
                pin=KEEP,
            )
        arrived.append(deliver(packed))
        if number >= 1:
            turn(number - 1)
    turn(len(sizes) - 1)
    aligned = [
        ([lax.ppermute(code, axes, across(step)) for step in range(1, groups)], *rows_of)
        for code, rows_of in zip(codes, kept)
    ]
    means = []
    gain = None
    hot, info = tables[2:]
    for number, (codes, sums, high, mid) in enumerate(aligned):
        first, last = number == 0, number == len(sizes) - 1
        kernel = functools.partial(score, parts, cap, groups - 1, first, last)
        outs = [(sums.shape, bf16)]
        outs += [((subs, LANES), f32)] if first else []
        outs += [((-(-parts // 8) * 8, LANES), f32) if last else ((8, rows), f32)]
        args = [*codes, sums, high, mid, hot, info]
        if first:
            mean, *rest = call(kernel, outs, *args)
            info = rest[0]
            gain = rest[1]
        else:
            mean, gain = call(kernel, outs, *args, gain)
        means.append(mean)
    returned = [gain]
    for part in range(1, parts):
        returned.append(lax.ppermute(gain, axes, [(b, a) for a, b in forward(part)]))
    (gains,) = call(functools.partial(unpack, parts), [((1, people), f32)], slot, *returned)
    mine = [
        lax.dynamic_slice_in_dim(mean, square * owned, owned).reshape(owned, 2, -1) for mean in means
    ]
    averages = jnp.concatenate(mine, axis=2)
    return averages, gains, info[0, 2] > 0.0


def shards(particles, classes, angles, counts):
    n_dom = lax.axis_size("dom")
    n_cls = lax.axis_size("cls")
    pair = 2 if n_dom % 2 == 0 else 1
    z = lax.axis_index("dom")
    people = particles.shape[0]
    owned = CLASSES // (n_dom * n_cls)
    subs = n_dom // pair * owned
    parts = pair * n_cls
    label = classes.reshape(1, people)
    mean_rows = people / parts
    most = min(CAP * subs, people + ROWS - 1) // ROWS * ROWS
    cap = min(most, -(-int(mean_rows + 2.0 * math.sqrt(mean_rows)) // ROWS) * ROWS)
    run = functools.partial(exchange, n_dom=n_dom, n_cls=n_cls, pair=pair)
    averages, gains, over = run(cap, particles, label, angles, counts, z // pair)
    if cap < most:
        averages, gains = lax.cond(
            over,
            lambda: run(most, particles, label, angles, counts, z // pair)[:2],
            lambda: (averages, gains),
        )
    n_coef = lax.axis_size("coef")
    total = gains
    for turn in range(1, n_coef):
        total = total + lax.ppermute(gains, "coef", [(i, (i + turn) % n_coef) for i in range(n_coef)])
    return averages, total.reshape(people)


def solution(mesh):
    in_specs = (
        P(("groups", "dom", "cls"), None, "coef"),
        P(("groups", "dom", "cls"), None),
        P(("groups", "dom", "cls")),
        P(("groups", "dom", "cls")),
    )
    out_specs = (P(("groups", "dom", "cls"), None, "coef"), P(("groups", "dom", "cls")))
    return jax.shard_map(shards, mesh=mesh, in_specs=in_specs, out_specs=out_specs, check_vma=False)
```
